32 devices in a mesh: logger: 4 (over y, x), seq: 2 (over core), vocab: 4 (over z).
Axes of the slice: x: 2, y: 2, z: 4, core: 2. Of those that a mesh axis runs over, the one named last changes fastest.
Arguments:
- hidden: bfloat16 [4, 64, 4096], P('logger', ('seq', 'vocab'))
- head_weight: bfloat16 [4, 4096, 4096], P('logger', None, ('seq', 'vocab')), may hold values from -0.09375 to 0.09375
- logged_tokens: int32 [64], replicated, may hold values from 0 to 4095
- logger_share: float32 [4], replicated, may hold values from 0.1 to 1
Outputs:
- log_weight: float32 [4, 64], P('logger', ('seq', 'vocab'))
The draws below stay inside these ranges and needn't reach their ends.
All inputs are finite; a program needn't handle non-finite values.
Results may differ from the reference program's by a relative error of at most 0.00045.
Values may be sent and summed in bfloat16 or wider, within the bound.
A program may use at most 64 MiB of HBM per device.

```python
import math
import jax
import jax.numpy as jnp
import numpy as np
from jax import lax

D = 4096
LOGGERS = 4
VOCAB = 4096
TOKENS = 64
N_SEQ = 2


def draw_hidden(key, part):
    base = jax.random.normal(key, (LOGGERS, TOKENS, D), jnp.float32)
    base = jnp.clip(3.0 * base, -18.0, 18.0)
    return base.astype(jnp.bfloat16)


def place_ends(values, stream_key, smallest, top_value):
    longest = values.shape.index(max(values.shape))
    spots = []
    for shift in (0, 1):
        where = [jax.random.randint(jax.random.fold_in(stream_key, axis), (), 0, length) for axis, length in enumerate(values.shape)]
        where[longest] = (where[longest] + shift) % values.shape[longest]
        spots.append(tuple(where))
    return values.at[spots[0]].set(smallest).at[spots[1]].set(top_value)


def level_of(stream_key, dims, pieces, least, high):
    def one(dim, shards_of):
        steps = jax.random.uniform(jax.random.fold_in(jax.random.fold_in(stream_key, 6), dim), (shards_of,), jnp.float32, least / len(pieces), high / len(pieces))
        return jnp.repeat(jnp.exp(steps), dims[dim] // shards_of).reshape((-1,) + (1,) * (len(dims) - dim - 1))

    gain = one(*pieces[0])
    for cut in pieces[1:]:
        gain = gain * one(*cut)
    return gain


def rank_bounds(number_of, lean):
    loads = [(1 << 20) // math.isqrt(rank ** lean) + 1 for rank in range(1, number_of + 1)]
    scale = 1 + sum(loads) // (1 << 30)
    return np.cumsum(np.array([max(1, weight // scale) for weight in loads]))


def ranked(rng, extent, count, skew):
    table = rank_bounds(count, skew)
    pick = jax.random.randint(jax.random.fold_in(rng, 1), extent, 0, int(table[count - 1]))
    standing = jnp.searchsorted(jnp.asarray(table, jnp.int32), pick, side="right")
    return jax.random.permutation(jax.random.fold_in(rng, 2), count)[standing].astype(jnp.int32)


def normal_values(own_key, shape, scale, most, cuts=(), dtype=jnp.bfloat16):
    result = jax.random.normal(own_key, shape, jnp.float32) * scale
    if len(cuts) > 0:
        result = level_of(own_key, shape, cuts, -0.22, 0.18) * result
    return jnp.clip(result, min=-most, max=most).astype(dtype)


def setup_inputs(seed: int = 0) -> dict:
    splits = jax.random.split(jax.random.key(seed), 5)
    return {
        "hidden": draw_hidden(jax.random.fold_in(splits[4], 71), 0),
        "head_weight": normal_values(splits[1], (LOGGERS, D, VOCAB), D ** -0.5, 0.09375, ((0, 4), (2, 8))),
        "logged_tokens": place_ends(ranked(splits[2], (TOKENS,), VOCAB, 2), jax.random.fold_in(splits[2], 3), 0, VOCAB - 1).astype(jnp.int32),
        "logger_share": jnp.clip(jnp.exp(jax.random.uniform(splits[3], (LOGGERS,), jnp.float32, math.log(0.1), math.log(1.0))), 0.1, 1.0),
    }


def token_logprob(token_rows, weight, wanted):
    logits = jnp.dot(token_rows, weight, preferred_element_type=jnp.float32)
    largest = jnp.max(logits, axis=1)
    total = jnp.sum(jnp.exp(logits - largest[:, None]), axis=1)
    picked = jnp.take_along_axis(logits, wanted[:, None], axis=1)[:, 0]
    return picked - largest - jnp.log(total)


def reference(hidden, head_weight, logged_tokens, logger_share):
    block_len = TOKENS // N_SEQ
    results = []
    for member in range(LOGGERS):
        weight = head_weight[member]

        def one_block(inputs_pair):
            return token_logprob(inputs_pair[0], weight, inputs_pair[1])

        blocks = lax.map(one_block, (hidden[member].reshape(N_SEQ, block_len, D), logged_tokens.reshape(N_SEQ, block_len)))
        results.append(blocks.reshape(TOKENS))
    logp = jnp.stack(results)
    counts = jnp.arange(1, TOKENS + 1).astype(jnp.float32)
    running = jnp.cumsum(logp, axis=1) / counts[None, :]
    prior = jnp.log(logger_share) - jnp.log(jnp.sum(logger_share))
    shifted = prior[:, None] + running
    highest = jnp.max(shifted, axis=0)
    mixture = highest + jnp.log(jnp.sum(jnp.exp(shifted - highest[None, :]), axis=0))
    return running - mixture[None, :]
```

```python
import functools

import jax
import jax.numpy as jnp
from jax import lax
from jax.experimental import pallas as pl
from jax.experimental.pallas import tpu as pltpu
from jax.sharding import PartitionSpec as P

MESH = pl.DeviceIdType.MESH
F32 = jnp.float32
CHUNKS = 2


def kernel(n_log, n_seq, n_voc, tok_ref, share_ref, hid_ref, w_ref, out_ref,
           gath, wv, acc, stat, load_sem, w_sem, recv_sem, up_sem, down_sem, side_sem, stat_send, stat_recv):
    my_l, my_s, z = lax.axis_index("logger"), lax.axis_index("seq"), lax.axis_index("vocab")
    group = n_seq * n_voc
    total = n_log * group
    per, depth = gath.shape[1], gath.shape[2]
    cols = wv.shape[1]
    tokens = group * per
    kc = depth // CHUNKS
    place = my_s * n_voc + z
    me = my_l * group + place

    def span(k):
        return pl.ds(k * kc, kc)

    own_load = pltpu.make_async_copy(hid_ref.at[0], gath.at[place], load_sem)
    own_load.start()
    w_loads = [pltpu.make_async_copy(w_ref.at[0, span(k)], wv.at[span(k)], w_sem.at[k]) for k in range(CHUNKS)]
    for copy in w_loads:
        copy.start()

    def coords(j):
        d = lax.rem(me + j, total)
        p = lax.rem(d, group)
        return (d // group, p // n_voc, lax.rem(p, n_voc)), d

    barrier = pltpu.get_barrier_semaphore()
    for j in range(1, total):
        pl.semaphore_signal(barrier, inc=1, device_id=coords(j)[0], device_id_type=MESH)

    row = lax.broadcasted_iota(jnp.int32, (tokens, tokens), 0)
    col = lax.broadcasted_iota(jnp.int32, (tokens, tokens), 1)
    tok = jnp.broadcast_to(tok_ref[...].astype(F32), (tokens, tokens))
    wanted = jnp.sum(jnp.where(row == col, tok, 0.0), axis=1, keepdims=True)
    wanted = wanted.astype(jnp.int32) - place * cols

    own_load.wait()
    pl.semaphore_wait(barrier, total - 1)

    def send(slot, k, sem, target):
        part = gath.at[slot, :, span(k)]
        return pltpu.make_async_remote_copy(
            src_ref=part, dst_ref=part, send_sem=sem.at[slot, k], recv_sem=recv_sem.at[slot, k],
            device_id=target, device_id_type=MESH)

    def up(slot, k):
        return send(slot, k, up_sem, (my_l, my_s, z + 1))

    def down(slot, k):
        return send(slot, k, down_sem, (my_l, my_s, z - 1))

    def side(slot, k, j):
        return send(slot, k, side_sem.at[j - 1], (my_l, lax.rem(my_s + j, n_seq), z))

    def relay(slot, k, go_up, go_down):
        if go_up:
            pl.when(z < n_voc - 1)(lambda: up(slot, k).start())
        if go_down:
            pl.when(z > 0)(lambda: down(slot, k).start())
        for j in range(1, n_seq):
            side(slot, k, j).start()

    for k in range(CHUNKS):
        relay(place, k, True, True)
    for s in range(1, n_voc):
        for k in range(CHUNKS):
            @pl.when(z - s >= 0)
            def _():
                up(place - s, k).wait_recv()
                relay(place - s, k, True, False)

            @pl.when(z + s < n_voc)
            def _():
                down(place + s, k).wait_recv()
                relay(place + s, k, False, True)

    for k in range(CHUNKS):
        for j in range(1, n_seq):
            other = lax.rem(my_s + j, n_seq) * n_voc
            for v in range(n_voc):
                side(other + v, k, j).wait_recv()
        w_loads[k].wait()
        lhs = gath[:, :, k * kc:(k + 1) * kc].astype(F32).reshape(tokens, kc).astype(jnp.bfloat16)
        part = jnp.dot(lhs, wv[k * kc:(k + 1) * kc, :], preferred_element_type=F32)
        if k == 0:
            acc[...] = part
        else:
            acc[...] += part

    logits = acc[...]
    top = jnp.max(logits, axis=1, keepdims=True)
    lse = top + jnp.log(jnp.sum(jnp.exp(logits - top), axis=1, keepdims=True))
    ids = lax.broadcasted_iota(jnp.int32, (tokens, cols), 1)
    pick = jnp.sum(jnp.where(ids == wanted, logits, 0.0), axis=1, keepdims=True)
    lane = lax.broadcasted_iota(jnp.int32, (tokens, 2 * tokens), 1)
    rows = lax.broadcasted_iota(jnp.int32, (tokens, 2 * tokens), 0)
    both = jnp.where(lane == rows, lse, 0.0) + jnp.where(lane == rows + tokens, pick, 0.0)
    stat[me] = jnp.sum(both, axis=0, keepdims=True)

    def stat_copy(j):
        target, _ = coords(j)
        return pltpu.make_async_remote_copy(
            src_ref=stat.at[me], dst_ref=stat.at[me], send_sem=stat_send.at[j], recv_sem=stat_recv.at[me],
            device_id=target, device_id_type=MESH)

    for j in range(1, total):
        stat_copy(j).start()

    for k in range(CHUNKS):
        pl.when(z < n_voc - 1)(lambda: up(place, k).wait_send())
        pl.when(z > 0)(lambda: down(place, k).wait_send())
        for j in range(1, n_seq):
            side(place, k, j).wait_send()
        for s in range(1, n_voc):
            @pl.when(z - s >= 0)
            def _():
                pl.when(z < n_voc - 1)(lambda: up(place - s, k).wait_send())
                for j in range(1, n_seq):
                    side(place - s, k, j).wait_send()

            @pl.when(z + s < n_voc)
            def _():
                pl.when(z > 0)(lambda: down(place + s, k).wait_send())
                for j in range(1, n_seq):
                    side(place + s, k, j).wait_send()

    prior = []
    whole = share_ref[0]
    for l in range(1, n_log):
        whole = whole + share_ref[l]
    for l in range(n_log):
        prior.append(jnp.log(jnp.full((per, 1), share_ref[l], F32)) - jnp.log(jnp.full((per, 1), whole, F32)))

    for j in range(1, total):
        _, d = coords(j)
        pltpu.make_async_remote_copy(
            src_ref=stat.at[d], dst_ref=stat.at[d], send_sem=stat_send.at[j], recv_sem=stat_recv.at[d],
            device_id=coords(j)[0], device_id_type=MESH).wait_recv()

    parts = stat[...].reshape(n_log, group, 2 * tokens)
    high = jnp.max(parts, axis=1, keepdims=True)
    lses = high + jnp.log(jnp.sum(jnp.exp(parts - high), axis=1, keepdims=True))
    picks = jnp.sum(parts, axis=1, keepdims=True)
    wide = lax.broadcasted_iota(jnp.int32, (n_log, 1, 2 * tokens), 2)
    signed = jnp.where(wide < tokens, -lses, picks)
    at = lax.broadcasted_iota(jnp.int32, (per, 2 * tokens), 1)
    at = jnp.where(at < tokens, at, at - tokens)
    limit = place * per + lax.broadcasted_iota(jnp.int32, (per, 2 * tokens), 0)
    keep = at <= limit
    counts = (place * per + 1 + lax.broadcasted_iota(jnp.int32, (per, 1), 0)).astype(F32)
    running = [jnp.sum(jnp.where(keep, signed[l], 0.0), axis=1, keepdims=True) / counts for l in range(n_log)]
    shifted = [prior[l] + running[l] for l in range(n_log)]
    highest = functools.reduce(jnp.maximum, shifted)
    mixture = highest + jnp.log(sum(jnp.exp(s - highest) for s in shifted))
    own = running[0]
    for l in range(1, n_log):
        own = jnp.where(my_l == l, running[l], own)
    r8 = lax.broadcasted_iota(jnp.int32, (per, per), 0)
    c8 = lax.broadcasted_iota(jnp.int32, (per, per), 1)
    out_ref[...] = jnp.sum(jnp.where(r8 == c8, own - mixture, 0.0), axis=0, keepdims=True)

    for j in range(1, total):
        stat_copy(j).wait_send()


def fused(sizes, hidden, head_weight, logged_tokens, logger_share):
    n_log, n_seq, n_voc = sizes
    group = n_seq * n_voc
    total = n_log * group
    per, depth = hidden.shape[1:]
    cols = head_weight.shape[2]
    tokens = logged_tokens.shape[0]
    vmem = pl.BlockSpec(memory_space=pltpu.VMEM)
    return pl.pallas_call(
        functools.partial(kernel, n_log, n_seq, n_voc),
        out_shape=jax.ShapeDtypeStruct((1, per), F32),
        in_specs=[vmem, pl.BlockSpec(memory_space=pltpu.SMEM),
                  pl.BlockSpec(memory_space=pltpu.HBM), pl.BlockSpec(memory_space=pltpu.HBM)],
        out_specs=vmem,
        scratch_shapes=[
            pltpu.VMEM((group, per, depth), jnp.bfloat16),
            pltpu.VMEM((depth, cols), jnp.bfloat16),
            pltpu.VMEM((tokens, cols), F32),
            pltpu.VMEM((total, 1, 2 * tokens), F32),
            pltpu.SemaphoreType.DMA,
            pltpu.SemaphoreType.DMA((CHUNKS,)),
            pltpu.SemaphoreType.DMA((group, CHUNKS)),
            pltpu.SemaphoreType.DMA((group, CHUNKS)),
            pltpu.SemaphoreType.DMA((group, CHUNKS)),
            pltpu.SemaphoreType.DMA((max(n_seq - 1, 1), group, CHUNKS)),
            pltpu.SemaphoreType.DMA((total,)),
            pltpu.SemaphoreType.DMA((total,)),
        ],
        compiler_params=pltpu.CompilerParams(
            collective_id=0, has_side_effects=True, vmem_limit_bytes=32 * 2**20),
    )(logged_tokens.reshape(1, tokens), logger_share, hidden, head_weight)


def general(hidden, head_weight, logged_tokens, logger_share):
    axes = ("seq", "vocab")
    weight = head_weight[0]
    cols, per = weight.shape[1], hidden.shape[1]
    tokens = logged_tokens.shape[0]
    place = lax.axis_index(axes)
    logits = jnp.dot(lax.all_gather(hidden[0], axes, axis=0, tiled=True), weight, preferred_element_type=F32)
    top = jnp.max(logits, axis=1)
    total = jnp.sum(jnp.exp(logits - top[:, None]), axis=1)
    ids = place * cols + lax.broadcasted_iota(jnp.int32, (1, cols), 1)
    pick = jnp.sum(jnp.where(logged_tokens[:, None] == ids, logits, 0.0), axis=1)
    whole = lax.pmax(top, axes)
    total, pick = lax.psum((total * jnp.exp(top - whole), pick), axes)
    logp = pick - whole - jnp.log(total)
    mine = place * per + lax.broadcasted_iota(jnp.int32, (per, 1), 0)
    before = lax.broadcasted_iota(jnp.int32, (1, tokens), 1) <= mine
    running = jnp.sum(jnp.where(before, logp[None, :], 0.0), axis=1) / (mine[:, 0] + 1).astype(F32)
    every = lax.all_gather(running[None, :], "logger", axis=0, tiled=True)
    prior = jnp.log(logger_share) - jnp.log(jnp.sum(logger_share))
    shifted = prior[:, None] + every
    high = jnp.max(shifted, axis=0)
    mixture = high + jnp.log(jnp.sum(jnp.exp(shifted - high[None, :]), axis=0))
    return (running - mixture)[None, :]


def solution(mesh):
    sizes = tuple(mesh.shape[a] for a in ("logger", "seq", "vocab"))

    def on_device(hidden, head_weight, logged_tokens, logger_share):
        small = sizes[1] * sizes[2] == 8 and 2 * logged_tokens.shape[0] == 128
        body = functools.partial(fused, sizes) if small else general
        return body(hidden, head_weight, logged_tokens, logger_share)

    return jax.shard_map(
        on_device,
        mesh=mesh,
        in_specs=(
            P("logger", ("seq", "vocab"), None),
            P("logger", None, ("seq", "vocab")),
            P(),
            P(),
        ),
        out_specs=P("logger", ("seq", "vocab")),
        check_vma=False,
    )
```

```python
import functools

import jax
import jax.numpy as jnp
from jax import lax
from jax.experimental import pallas as pl
from jax.experimental.pallas import tpu as pltpu
from jax.sharding import PartitionSpec as P

MESH = pl.DeviceIdType.MESH
F32 = jnp.float32
CHUNKS = 2


def kernel(n_log, n_seq, n_voc, tok_ref, share_ref, hid_ref, w_ref, out_ref,
           gath, wv, acc, pair, stat, tok_v, share_v, load_sem, w_sem, recv_sem, far_sem, side_sem,
           pair_send, pair_recv, stat_send, stat_recv):
    my_l, my_s, z = lax.axis_index("logger"), lax.axis_index("seq"), lax.axis_index("vocab")
    group = n_seq * n_voc
    per, depth = gath.shape[1], gath.shape[2]
    cols = wv.shape[1]
    tokens = group * per
    kc = depth // CHUNKS
    place = my_s * n_voc + z
    logs = [my_l] + [lax.rem(my_l + i, n_log) for i in range(1, n_log)]
    seqs = [my_s] + [lax.rem(my_s + a, n_seq) for a in range(1, n_seq)]
    vocs = [z] + [lax.rem(z + b, n_voc) for b in range(1, n_voc)]
    chips = [(i, b) for i in range(n_log) for b in range(n_voc) if i or b]

    barrier = pltpu.get_barrier_semaphore()
    for i, b in chips:
        pl.semaphore_signal(barrier, inc=1, device_id=(logs[i], my_s, vocs[b]), device_id_type=MESH)
    for a in range(1, n_seq):
        pl.semaphore_signal(barrier, inc=1, device_id=(my_l, seqs[a], z), device_id_type=MESH)

    def span(k):
        return pl.ds(k * kc, kc)

    own_load = pltpu.make_async_copy(hid_ref.at[0], gath.at[place], load_sem.at[0])
    tok_load = pltpu.make_async_copy(tok_ref, tok_v, load_sem.at[1])
    share_load = pltpu.make_async_copy(share_ref, share_v, load_sem.at[2])
    w_loads = [pltpu.make_async_copy(w_ref.at[0, span(k)], wv.at[span(k)], w_sem.at[k]) for k in range(CHUNKS)]
    own_load.start()
    tok_load.start()
    share_load.start()
    for copy in w_loads:
        copy.start()
    own_load.wait()
    pl.semaphore_wait(barrier, len(chips) + n_seq - 1)

    def send(src, slot, k, sem, target):
        return pltpu.make_async_remote_copy(
            src_ref=src, dst_ref=gath.at[slot, :, span(k)], send_sem=sem, recv_sem=recv_sem.at[slot, k],
            device_id=target, device_id_type=MESH)

    def rows_of(slot, k):
        return gath.at[slot, :, span(k)]

    def far(b, k):
        return send(rows_of(place, k), place, k, far_sem.at[b - 1, k], (my_l, my_s, vocs[b]))

    def side(a, b, k):
        slot = my_s * n_voc + vocs[b]
        return send(rows_of(slot, k), slot, k, side_sem.at[a - 1, b, k], (my_l, seqs[a], z))

    def arrived(a, b, k):
        slot = seqs[a] * n_voc + vocs[b]
        send(rows_of(slot, k), slot, k, far_sem.at[0, k], (my_l, my_s, z)).wait_recv()

    for k in range(CHUNKS):
        for b in range(1, n_voc):
            far(b, k).start()
        for a in range(1, n_seq):
            side(a, 0, k).start()

    tok_load.wait()
    share_load.wait()
    row = lax.broadcasted_iota(jnp.int32, (tokens, tokens), 0)
    col = lax.broadcasted_iota(jnp.int32, (tokens, tokens), 1)
    tok = jnp.broadcast_to(tok_v[...].astype(F32), (tokens, tokens))
    wanted = jnp.sum(jnp.where(row == col, tok, 0.0), axis=1, keepdims=True)
    wanted = wanted.astype(jnp.int32) - place * cols
    whole = share_v[0]
    for l in range(1, n_log):
        whole = whole + share_v[l]
    prior = [jnp.log(jnp.full((per, 2 * tokens), share_v[l], F32)) - jnp.log(jnp.full((per, 2 * tokens), whole, F32))
             for l in range(n_log)]

    for k in range(CHUNKS):
        for b in range(1, n_voc):
            arrived(0, b, k)
            for a in range(1, n_seq):
                side(a, b, k).start()

    for k in range(CHUNKS):
        for a in range(1, n_seq):
            for b in range(n_voc):
                arrived(a, b, k)
        w_loads[k].wait()
        lhs = gath[:, :, k * kc:(k + 1) * kc].astype(F32).reshape(tokens, kc).astype(jnp.bfloat16)
        part = jnp.dot(lhs, wv[k * kc:(k + 1) * kc, :], preferred_element_type=F32)
        if k == 0:
            acc[...] = part
        else:
            acc[...] += part

    logits = acc[...]
    top = jnp.max(logits, axis=1, keepdims=True)
    lse = top + jnp.log(jnp.sum(jnp.exp(logits - top), axis=1, keepdims=True))
    ids = lax.broadcasted_iota(jnp.int32, (tokens, cols), 1)
    pick = jnp.sum(jnp.where(ids == wanted, logits, 0.0), axis=1, keepdims=True)
    lane = lax.broadcasted_iota(jnp.int32, (tokens, 2 * tokens), 1)
    rows = lax.broadcasted_iota(jnp.int32, (tokens, 2 * tokens), 0)
    both = jnp.where(lane == rows, lse, 0.0) + jnp.where(lane == rows + tokens, pick, 0.0)
    pair[my_s] = jnp.sum(both, axis=0, keepdims=True)

    def pair_copy(a, slot):
        return pltpu.make_async_remote_copy(
            src_ref=pair.at[slot], dst_ref=pair.at[slot], send_sem=pair_send.at[a], recv_sem=pair_recv.at[slot],
            device_id=(my_l, seqs[a], z), device_id_type=MESH)

    for a in range(1, n_seq):
        pair_copy(a, my_s).start()
    for a in range(1, n_seq):
        pair_copy(a, seqs[a]).wait_recv()

    def merged(parts, axis):
        high = jnp.max(parts, axis=axis, keepdims=True)
        lses = high + jnp.log(jnp.sum(jnp.exp(parts - high), axis=axis, keepdims=True))
        return lses, jnp.sum(parts, axis=axis, keepdims=True)

    wide = lax.broadcasted_iota(jnp.int32, (1, 1, 2 * tokens), 2)
    lses, picks = merged(pair[...], 0)
    me = my_l * n_voc + z
    stat[me] = jnp.where(wide < tokens, lses, picks)[0]

    def stat_copy(n, slot):
        return pltpu.make_async_remote_copy(
            src_ref=stat.at[slot], dst_ref=stat.at[slot], send_sem=stat_send.at[n], recv_sem=stat_recv.at[slot],
            device_id=(logs[chips[n][0]], my_s, vocs[chips[n][1]]), device_id_type=MESH)

    for n in range(len(chips)):
        stat_copy(n, me).start()

    for k in range(CHUNKS):
        for b in range(1, n_voc):
            far(b, k).wait_send()
        for a in range(1, n_seq):
            for b in range(n_voc):
                side(a, b, k).wait_send()
    for a in range(1, n_seq):
        pair_copy(a, my_s).wait_send()
    at = lax.broadcasted_iota(jnp.int32, (per, 2 * tokens), 1)
    at = jnp.where(at < tokens, at, at - tokens)
    index = place * per + lax.broadcasted_iota(jnp.int32, (per, 2 * tokens), 0)
    keep = at <= index
    counts = (index + 1).astype(F32)
    for n, (i, b) in enumerate(chips):
        stat_copy(n, logs[i] * n_voc + vocs[b]).wait_recv()

    lses, picks = merged(stat[...].reshape(n_log, n_voc, 2 * tokens), 1)
    signed = jnp.where(wide < tokens, -lses, picks)
    running = [jnp.sum(jnp.where(keep, signed[l], 0.0), axis=1, keepdims=True) / counts for l in range(n_log)]
    shifted = [prior[l] + running[l] for l in range(n_log)]
    highest = functools.reduce(jnp.maximum, shifted)
    mixture = highest + jnp.log(sum(jnp.exp(s - highest) for s in shifted))
    mine = running[0]
    for l in range(1, n_log):
        mine = jnp.where(my_l == l, running[l], mine)
    r8 = lax.broadcasted_iota(jnp.int32, (per, 2 * tokens), 0)
    c8 = lax.broadcasted_iota(jnp.int32, (per, 2 * tokens), 1)
    result = jnp.sum(jnp.where(r8 == c8, mine - mixture, 0.0), axis=0, keepdims=True)
    out_ref[...] = result[:, :per]

    for n in range(len(chips)):
        stat_copy(n, me).wait_send()


def fused(sizes, hidden, head_weight, logged_tokens, logger_share):
    n_log, n_seq, n_voc = sizes
    group = n_seq * n_voc
    per, depth = hidden.shape[1:]
    cols = head_weight.shape[2]
    tokens = logged_tokens.shape[0]
    vmem = pl.BlockSpec(memory_space=pltpu.VMEM)
    return pl.pallas_call(
        functools.partial(kernel, n_log, n_seq, n_voc),
        out_shape=pltpu.VMEM((1, per), F32),
        in_specs=[pl.BlockSpec(memory_space=pltpu.HBM)] * 4,
        out_specs=vmem,
        scratch_shapes=[
            pltpu.VMEM((group, per, depth), jnp.bfloat16),
            pltpu.VMEM((depth, cols), jnp.bfloat16),
            pltpu.VMEM((tokens, cols), F32),
            pltpu.VMEM((n_seq, 1, 2 * tokens), F32),
            pltpu.VMEM((n_log * n_voc, 1, 2 * tokens), F32),
            pltpu.VMEM((1, tokens), jnp.int32),
            pltpu.SMEM((n_log,), F32),
            pltpu.SemaphoreType.DMA((3,)),
            pltpu.SemaphoreType.DMA((CHUNKS,)),
            pltpu.SemaphoreType.DMA((group, CHUNKS)),
            pltpu.SemaphoreType.DMA((n_voc - 1, CHUNKS)),
            pltpu.SemaphoreType.DMA((n_seq - 1, n_voc, CHUNKS)),
            pltpu.SemaphoreType.DMA((n_seq,)),
            pltpu.SemaphoreType.DMA((n_seq,)),
            pltpu.SemaphoreType.DMA((n_log * n_voc,)),
            pltpu.SemaphoreType.DMA((n_log * n_voc,)),
        ],
        compiler_params=pltpu.CompilerParams(
            collective_id=0, has_side_effects=True, vmem_limit_bytes=63 * 2**20),
    )(logged_tokens.reshape(1, tokens), logger_share, hidden, head_weight)


def general(hidden, head_weight, logged_tokens, logger_share):
    axes = ("seq", "vocab")
    weight = head_weight[0]
    cols, per = weight.shape[1], hidden.shape[1]
    tokens = logged_tokens.shape[0]
    place = lax.axis_index(axes)
    logits = jnp.dot(lax.all_gather(hidden[0], axes, axis=0, tiled=True), weight, preferred_element_type=F32)
    top = jnp.max(logits, axis=1)
    total = jnp.sum(jnp.exp(logits - top[:, None]), axis=1)
    ids = place * cols + lax.broadcasted_iota(jnp.int32, (1, cols), 1)
    pick = jnp.sum(jnp.where(logged_tokens[:, None] == ids, logits, 0.0), axis=1)
    whole = lax.pmax(top, axes)
    total, pick = lax.psum((total * jnp.exp(top - whole), pick), axes)
    logp = pick - whole - jnp.log(total)
    mine = place * per + lax.broadcasted_iota(jnp.int32, (per, 1), 0)
    before = lax.broadcasted_iota(jnp.int32, (1, tokens), 1) <= mine
    running = jnp.sum(jnp.where(before, logp[None, :], 0.0), axis=1) / (mine[:, 0] + 1).astype(F32)
    every = lax.all_gather(running[None, :], "logger", axis=0, tiled=True)
    prior = jnp.log(logger_share) - jnp.log(jnp.sum(logger_share))
    shifted = prior[:, None] + every
    high = jnp.max(shifted, axis=0)
    mixture = high + jnp.log(jnp.sum(jnp.exp(shifted - high[None, :]), axis=0))
    return (running - mixture)[None, :]


def solution(mesh):
    sizes = tuple(mesh.shape[a] for a in ("logger", "seq", "vocab"))

    def on_device(hidden, head_weight, logged_tokens, logger_share):
        small = sizes[1:] == (2, 4) and 2 * logged_tokens.shape[0] == 128
        body = functools.partial(fused, sizes) if small else general
        return body(hidden, head_weight, logged_tokens, logger_share)

    return jax.shard_map(
        on_device,
        mesh=mesh,
        in_specs=(
            P("logger", ("seq", "vocab"), None),
            P("logger", None, ("seq", "vocab")),
            P(),
            P(),
        ),
        out_specs=P("logger", ("seq", "vocab")),
        check_vma=False,
    )
```

```python
import functools

import jax
import jax.numpy as jnp
from jax import lax
from jax.experimental import pallas as pl
from jax.experimental.pallas import tpu as pltpu
from jax.sharding import PartitionSpec as P

MESH = pl.DeviceIdType.MESH
F32 = jnp.float32
CHUNKS = 2
RELAYED = (0,)


def kernel(n_log, n_seq, n_voc, tok_ref, share_ref, hid_ref, w_ref, out_ref,
           gath, wv, acc, pair, stat, tok_v, share_v, load_sem, w_sem, recv_sem, far_sem, side_sem,
           pair_send, pair_recv, stat_send, stat_recv):
    my_l, my_s, z = lax.axis_index("logger"), lax.axis_index("seq"), lax.axis_index("vocab")
    group = n_seq * n_voc
    per, depth = gath.shape[1], gath.shape[2]
    cols = wv.shape[1]
    tokens = group * per
    kc = depth // CHUNKS
    place = my_s * n_voc + z
    logs = [my_l] + [lax.rem(my_l + i, n_log) for i in range(1, n_log)]
    seqs = [my_s] + [lax.rem(my_s + a, n_seq) for a in range(1, n_seq)]
    half = z // 2
    vocs = [z, lax.rem(z + 1 + 2 * half, n_voc), lax.rem(z + 2, n_voc), lax.rem(z + 3 - 2 * half, n_voc)]
    inner = (z > 0) & (z < n_voc - 1)
    outer = (z == 0) | (z == n_voc - 1)
    chips = [(i, b) for i in range(n_log) for b in range(n_voc) if i or b]

    barrier = pltpu.get_barrier_semaphore()
    for i, b in chips:
        pl.semaphore_signal(barrier, inc=1, device_id=(logs[i], my_s, vocs[b]), device_id_type=MESH)
    for a in range(1, n_seq):
        pl.semaphore_signal(barrier, inc=1, device_id=(my_l, seqs[a], z), device_id_type=MESH)

    def span(k):
        return pl.ds(k * kc, kc)

    own_load = pltpu.make_async_copy(hid_ref.at[0], gath.at[place], load_sem.at[0])
    tok_load = pltpu.make_async_copy(tok_ref, tok_v, load_sem.at[1])
    share_load = pltpu.make_async_copy(share_ref, share_v, load_sem.at[2])
    w_loads = [pltpu.make_async_copy(w_ref.at[0, span(k)], wv.at[span(k)], w_sem.at[k]) for k in range(CHUNKS)]
    own_load.start()
    tok_load.start()
    share_load.start()
    for copy in w_loads:
        copy.start()
    own_load.wait()
    pl.semaphore_wait(barrier, len(chips) + n_seq - 1)

    def send(src, slot, k, sem, target):
        return pltpu.make_async_remote_copy(
            src_ref=src, dst_ref=gath.at[slot, :, span(k)], send_sem=sem, recv_sem=recv_sem.at[slot, k],
            device_id=target, device_id_type=MESH)

    def rows_of(slot, k):
        return gath.at[slot, :, span(k)]

    def far(b, k):
        return send(rows_of(place, k), place, k, far_sem.at[b - 1, k], (my_l, my_s, vocs[b]))

    def passed(k):
        slot = my_s * n_voc + vocs[1]
        return send(rows_of(slot, k), slot, k, far_sem.at[1, k], (my_l, my_s, vocs[3]))

    def side(a, b, k):
        slot = my_s * n_voc + vocs[b]
        return send(rows_of(slot, k), slot, k, side_sem.at[a - 1, b, k], (my_l, seqs[a], z))

    def arrived(a, b, k):
        slot = seqs[a] * n_voc + vocs[b]
        send(rows_of(slot, k), slot, k, far_sem.at[0, k], (my_l, my_s, z)).wait_recv()

    for k in range(CHUNKS):
        for b in (1, 2, 3):
            if b == 2 and k in RELAYED:
                pl.when(outer)(lambda: far(2, k).start())
            else:
                far(b, k).start()
        for a in range(1, n_seq):
            side(a, 0, k).start()

    tok_load.wait()
    share_load.wait()
    row = lax.broadcasted_iota(jnp.int32, (tokens, tokens), 0)
    col = lax.broadcasted_iota(jnp.int32, (tokens, tokens), 1)
    tok = jnp.broadcast_to(tok_v[...].astype(F32), (tokens, tokens))
    wanted = jnp.sum(jnp.where(row == col, tok, 0.0), axis=1, keepdims=True)
    wanted = wanted.astype(jnp.int32) - place * cols
    whole = share_v[0]
    for l in range(1, n_log):
        whole = whole + share_v[l]
    prior = [jnp.log(jnp.full((per, 2 * tokens), share_v[l], F32)) - jnp.log(jnp.full((per, 2 * tokens), whole, F32))
             for l in range(n_log)]

    for k in range(CHUNKS):
        for b in range(1, n_voc):
            arrived(0, b, k)
            if b == 1 and k in RELAYED:
                pl.when(inner)(lambda: passed(k).start())
            for a in range(1, n_seq):
                side(a, b, k).start()

    for k in range(CHUNKS):
        for a in range(1, n_seq):
            for b in range(n_voc):
                arrived(a, b, k)
        w_loads[k].wait()
        lhs = gath[:, :, k * kc:(k + 1) * kc].astype(F32).reshape(tokens, kc).astype(jnp.bfloat16)
        part = jnp.dot(lhs, wv[k * kc:(k + 1) * kc, :], preferred_element_type=F32)
        if k == 0:
            acc[...] = part
        else:
            acc[...] += part

    logits = acc[...]
    top = jnp.max(logits, axis=1, keepdims=True)
    lse = top + jnp.log(jnp.sum(jnp.exp(logits - top), axis=1, keepdims=True))
    ids = lax.broadcasted_iota(jnp.int32, (tokens, cols), 1)
    pick = jnp.sum(jnp.where(ids == wanted, logits, 0.0), axis=1, keepdims=True)
    lane = lax.broadcasted_iota(jnp.int32, (tokens, 2 * tokens), 1)
    rows = lax.broadcasted_iota(jnp.int32, (tokens, 2 * tokens), 0)
    both = jnp.where(lane == rows, lse, 0.0) + jnp.where(lane == rows + tokens, pick, 0.0)
    pair[my_s] = jnp.sum(both, axis=0, keepdims=True)

    def pair_copy(a, slot):
        return pltpu.make_async_remote_copy(
            src_ref=pair.at[slot], dst_ref=pair.at[slot], send_sem=pair_send.at[a], recv_sem=pair_recv.at[slot],
            device_id=(my_l, seqs[a], z), device_id_type=MESH)

    for a in range(1, n_seq):
        pair_copy(a, my_s).start()
    for a in range(1, n_seq):
        pair_copy(a, seqs[a]).wait_recv()

    def merged(parts, axis):
        high = jnp.max(parts, axis=axis, keepdims=True)
        lses = high + jnp.log(jnp.sum(jnp.exp(parts - high), axis=axis, keepdims=True))
        return lses, jnp.sum(parts, axis=axis, keepdims=True)

    wide = lax.broadcasted_iota(jnp.int32, (1, 1, 2 * tokens), 2)
    lses, picks = merged(pair[...], 0)
    me = my_l * n_voc + z
    stat[me] = jnp.where(wide < tokens, lses, picks)[0]

    def stat_copy(n, slot):
        return pltpu.make_async_remote_copy(
            src_ref=stat.at[slot], dst_ref=stat.at[slot], send_sem=stat_send.at[n], recv_sem=stat_recv.at[slot],
            device_id=(logs[chips[n][0]], my_s, vocs[chips[n][1]]), device_id_type=MESH)

    for n in range(len(chips)):
        stat_copy(n, me).start()

    for k in range(CHUNKS):
        for b in range(1, n_voc):
            if b == 2 and k in RELAYED:
                pl.when(outer)(lambda: far(2, k).wait_send())
                pl.when(inner)(lambda: passed(k).wait_send())
            else:
                far(b, k).wait_send()
        for a in range(1, n_seq):
            for b in range(n_voc):
                side(a, b, k).wait_send()
    for a in range(1, n_seq):
        pair_copy(a, my_s).wait_send()
    at = lax.broadcasted_iota(jnp.int32, (per, 2 * tokens), 1)
    at = jnp.where(at < tokens, at, at - tokens)
    index = place * per + lax.broadcasted_iota(jnp.int32, (per, 2 * tokens), 0)
    keep = at <= index
    counts = (index + 1).astype(F32)
    for n, (i, b) in enumerate(chips):
        stat_copy(n, logs[i] * n_voc + vocs[b]).wait_recv()

    lses, picks = merged(stat[...].reshape(n_log, n_voc, 2 * tokens), 1)
    signed = jnp.where(wide < tokens, -lses, picks)
    running = [jnp.sum(jnp.where(keep, signed[l], 0.0), axis=1, keepdims=True) / counts for l in range(n_log)]
    shifted = [prior[l] + running[l] for l in range(n_log)]
    highest = functools.reduce(jnp.maximum, shifted)
    mixture = highest + jnp.log(sum(jnp.exp(s - highest) for s in shifted))
    mine = running[0]
    for l in range(1, n_log):
        mine = jnp.where(my_l == l, running[l], mine)
    r8 = lax.broadcasted_iota(jnp.int32, (per, 2 * tokens), 0)
    c8 = lax.broadcasted_iota(jnp.int32, (per, 2 * tokens), 1)
    result = jnp.sum(jnp.where(r8 == c8, mine - mixture, 0.0), axis=0, keepdims=True)
    out_ref[...] = result[:, :per]

    for n in range(len(chips)):
        stat_copy(n, me).wait_send()


def fused(sizes, hidden, head_weight, logged_tokens, logger_share):
    n_log, n_seq, n_voc = sizes
    group = n_seq * n_voc
    per, depth = hidden.shape[1:]
    cols = head_weight.shape[2]
    tokens = logged_tokens.shape[0]
    vmem = pl.BlockSpec(memory_space=pltpu.VMEM)
    return pl.pallas_call(
        functools.partial(kernel, n_log, n_seq, n_voc),
        out_shape=pltpu.VMEM((1, per), F32),
        in_specs=[pl.BlockSpec(memory_space=pltpu.HBM)] * 4,
        out_specs=vmem,
        scratch_shapes=[
            pltpu.VMEM((group, per, depth), jnp.bfloat16),
            pltpu.VMEM((depth, cols), jnp.bfloat16),
            pltpu.VMEM((tokens, cols), F32),
            pltpu.VMEM((n_seq, 1, 2 * tokens), F32),
            pltpu.VMEM((n_log * n_voc, 1, 2 * tokens), F32),
            pltpu.VMEM((1, tokens), jnp.int32),
            pltpu.SMEM((n_log,), F32),
            pltpu.SemaphoreType.DMA((3,)),
            pltpu.SemaphoreType.DMA((CHUNKS,)),
            pltpu.SemaphoreType.DMA((group, CHUNKS)),
            pltpu.SemaphoreType.DMA((n_voc - 1, CHUNKS)),
            pltpu.SemaphoreType.DMA((n_seq - 1, n_voc, CHUNKS)),
            pltpu.SemaphoreType.DMA((n_seq,)),
            pltpu.SemaphoreType.DMA((n_seq,)),
            pltpu.SemaphoreType.DMA((n_log * n_voc,)),
            pltpu.SemaphoreType.DMA((n_log * n_voc,)),
        ],
        compiler_params=pltpu.CompilerParams(
            collective_id=0, has_side_effects=True, vmem_limit_bytes=63 * 2**20),
    )(logged_tokens.reshape(1, tokens), logger_share, hidden, head_weight)


def general(hidden, head_weight, logged_tokens, logger_share):
    axes = ("seq", "vocab")
    weight = head_weight[0]
    cols, per = weight.shape[1], hidden.shape[1]
    tokens = logged_tokens.shape[0]
    place = lax.axis_index(axes)
    logits = jnp.dot(lax.all_gather(hidden[0], axes, axis=0, tiled=True), weight, preferred_element_type=F32)
    top = jnp.max(logits, axis=1)
    total = jnp.sum(jnp.exp(logits - top[:, None]), axis=1)
    ids = place * cols + lax.broadcasted_iota(jnp.int32, (1, cols), 1)
    pick = jnp.sum(jnp.where(logged_tokens[:, None] == ids, logits, 0.0), axis=1)
    whole = lax.pmax(top, axes)
    total, pick = lax.psum((total * jnp.exp(top - whole), pick), axes)
    logp = pick - whole - jnp.log(total)
    mine = place * per + lax.broadcasted_iota(jnp.int32, (per, 1), 0)
    before = lax.broadcasted_iota(jnp.int32, (1, tokens), 1) <= mine
    running = jnp.sum(jnp.where(before, logp[None, :], 0.0), axis=1) / (mine[:, 0] + 1).astype(F32)
    every = lax.all_gather(running[None, :], "logger", axis=0, tiled=True)
    prior = jnp.log(logger_share) - jnp.log(jnp.sum(logger_share))
    shifted = prior[:, None] + every
    high = jnp.max(shifted, axis=0)
    mixture = high + jnp.log(jnp.sum(jnp.exp(shifted - high[None, :]), axis=0))
    return (running - mixture)[None, :]


def solution(mesh):
    sizes = tuple(mesh.shape[a] for a in ("logger", "seq", "vocab"))

    def on_device(hidden, head_weight, logged_tokens, logger_share):
        small = sizes[1:] == (2, 4) and 2 * logged_tokens.shape[0] == 128
        body = functools.partial(fused, sizes) if small else general
        return body(hidden, head_weight, logged_tokens, logger_share)

    return jax.shard_map(
        on_device,
        mesh=mesh,
        in_specs=(
            P("logger", ("seq", "vocab"), None),
            P("logger", None, ("seq", "vocab")),
            P(),
            P(),
        ),
        out_specs=P("logger", ("seq", "vocab")),
        check_vma=False,
    )
```

```python
import functools

import jax
import jax.numpy as jnp
from jax import lax
from jax.experimental import pallas as pl
from jax.experimental.pallas import tpu as pltpu
from jax.sharding import PartitionSpec as P

MESH = pl.DeviceIdType.MESH
F32 = jnp.float32
CHUNKS = 2
EDGES = (0, 3, 8)
RELAYED = (0,)


def kernel(n_log, n_seq, n_voc, tok_ref, share_ref, hid_ref, w_ref, out_ref,
           gath, wv, acc, pair, stat, tok_v, share_v, load_sem, w_sem, recv_sem, far_sem, side_sem,
           pair_send, pair_recv, stat_send, stat_recv):
    my_l, my_s, z = lax.axis_index("logger"), lax.axis_index("seq"), lax.axis_index("vocab")
    group = n_seq * n_voc
    per, depth = gath.shape[1], gath.shape[2]
    cols = wv.shape[1]
    tokens = group * per
    edges = [depth * part // 8 for part in EDGES]
    place = my_s * n_voc + z
    logs = [my_l] + [lax.rem(my_l + i, n_log) for i in range(1, n_log)]
    seqs = [my_s] + [lax.rem(my_s + a, n_seq) for a in range(1, n_seq)]
    half = z // 2
    vocs = [z, lax.rem(z + 1 + 2 * half, n_voc), lax.rem(z + 2, n_voc), lax.rem(z + 3 - 2 * half, n_voc)]
    inner = (z > 0) & (z < n_voc - 1)
    outer = (z == 0) | (z == n_voc - 1)
    chips = [(i, b) for i in range(n_log) for b in range(n_voc) if i or b]

    barrier = pltpu.get_barrier_semaphore()
    for i, b in chips:
        pl.semaphore_signal(barrier, inc=1, device_id=(logs[i], my_s, vocs[b]), device_id_type=MESH)
    for a in range(1, n_seq):
        pl.semaphore_signal(barrier, inc=1, device_id=(my_l, seqs[a], z), device_id_type=MESH)

    def span(k):
        return pl.ds(edges[k], edges[k + 1] - edges[k])

    own_load = pltpu.make_async_copy(hid_ref.at[0], gath.at[place], load_sem.at[0])
    tok_load = pltpu.make_async_copy(tok_ref, tok_v, load_sem.at[1])
    share_load = pltpu.make_async_copy(share_ref, share_v, load_sem.at[2])
    w_loads = [pltpu.make_async_copy(w_ref.at[0, span(k)], wv.at[span(k)], w_sem.at[k]) for k in range(CHUNKS)]
    own_load.start()
    tok_load.start()
    share_load.start()
    for copy in w_loads:
        copy.start()
    own_load.wait()
    pl.semaphore_wait(barrier, len(chips) + n_seq - 1)

    def send(src, slot, k, sem, target):
        return pltpu.make_async_remote_copy(
            src_ref=src, dst_ref=gath.at[slot, :, span(k)], send_sem=sem, recv_sem=recv_sem.at[slot, k],
            device_id=target, device_id_type=MESH)

    def rows_of(slot, k):
        return gath.at[slot, :, span(k)]

    def far(b, k):
        return send(rows_of(place, k), place, k, far_sem.at[b - 1, k], (my_l, my_s, vocs[b]))

    def passed(k):
        slot = my_s * n_voc + vocs[1]
        return send(rows_of(slot, k), slot, k, far_sem.at[1, k], (my_l, my_s, vocs[3]))

    def side(a, b, k):
        slot = my_s * n_voc + vocs[b]
        return send(rows_of(slot, k), slot, k, side_sem.at[a - 1, b, k], (my_l, seqs[a], z))

    def arrived(a, b, k):
        slot = seqs[a] * n_voc + vocs[b]
        send(rows_of(slot, k), slot, k, far_sem.at[0, k], (my_l, my_s, z)).wait_recv()

    for k in range(CHUNKS):
        for b in (1, 2, 3):
            if b == 2 and k in RELAYED:
                pl.when(outer)(lambda: far(2, k).start())
            else:
                far(b, k).start()
        for a in range(1, n_seq):
            side(a, 0, k).start()

    tok_load.wait()
    share_load.wait()
    row = lax.broadcasted_iota(jnp.int32, (tokens, tokens), 0)
    col = lax.broadcasted_iota(jnp.int32, (tokens, tokens), 1)
    tok = jnp.broadcast_to(tok_v[...].astype(F32), (tokens, tokens))
    wanted = jnp.sum(jnp.where(row == col, tok, 0.0), axis=1, keepdims=True)
    wanted = wanted.astype(jnp.int32) - place * cols
    whole = share_v[0]
    for l in range(1, n_log):
        whole = whole + share_v[l]
    prior = [jnp.log(jnp.full((per, 2 * tokens), share_v[l], F32)) - jnp.log(jnp.full((per, 2 * tokens), whole, F32))
             for l in range(n_log)]

    for k in range(CHUNKS):
        for b in range(1, n_voc):
            arrived(0, b, k)
            if b == 1 and k in RELAYED:
                pl.when(inner)(lambda: passed(k).start())
            for a in range(1, n_seq):
                side(a, b, k).start()

    for k in range(CHUNKS):
        for a in range(1, n_seq):
            for b in range(n_voc):
                arrived(a, b, k)
        w_loads[k].wait()
        lhs = gath[:, :, edges[k]:edges[k + 1]].astype(F32).reshape(tokens, edges[k + 1] - edges[k]).astype(jnp.bfloat16)
        part = jnp.dot(lhs, wv[edges[k]:edges[k + 1], :], preferred_element_type=F32)
        if k == 0:
            acc[...] = part
        else:
            acc[...] += part

    logits = acc[...]
    top = jnp.max(logits, axis=1, keepdims=True)
    lse = top + jnp.log(jnp.sum(jnp.exp(logits - top), axis=1, keepdims=True))
    ids = lax.broadcasted_iota(jnp.int32, (tokens, cols), 1)
    pick = jnp.sum(jnp.where(ids == wanted, logits, 0.0), axis=1, keepdims=True)
    lane = lax.broadcasted_iota(jnp.int32, (tokens, 2 * tokens), 1)
    rows = lax.broadcasted_iota(jnp.int32, (tokens, 2 * tokens), 0)
    both = jnp.where(lane == rows, lse, 0.0) + jnp.where(lane == rows + tokens, pick, 0.0)
    pair[my_s] = jnp.sum(both, axis=0, keepdims=True)

    def pair_copy(a, slot):
        return pltpu.make_async_remote_copy(
            src_ref=pair.at[slot], dst_ref=pair.at[slot], send_sem=pair_send.at[a], recv_sem=pair_recv.at[slot],
            device_id=(my_l, seqs[a], z), device_id_type=MESH)

    for a in range(1, n_seq):
        pair_copy(a, my_s).start()
    for a in range(1, n_seq):
        pair_copy(a, seqs[a]).wait_recv()

    def merged(parts, axis):
        high = jnp.max(parts, axis=axis, keepdims=True)
        lses = high + jnp.log(jnp.sum(jnp.exp(parts - high), axis=axis, keepdims=True))
        return lses, jnp.sum(parts, axis=axis, keepdims=True)

    wide = lax.broadcasted_iota(jnp.int32, (1, 1, 2 * tokens), 2)
    lses, picks = merged(pair[...], 0)
    me = my_l * n_voc + z
    stat[me] = jnp.where(wide < tokens, lses, picks)[0]

    def stat_copy(n, slot):
        return pltpu.make_async_remote_copy(
            src_ref=stat.at[slot], dst_ref=stat.at[slot], send_sem=stat_send.at[n], recv_sem=stat_recv.at[slot],
            device_id=(logs[chips[n][0]], my_s, vocs[chips[n][1]]), device_id_type=MESH)

    for n in reversed(range(len(chips))):
        stat_copy(n, me).start()

    for k in range(CHUNKS):
        for b in range(1, n_voc):
            if b == 2 and k in RELAYED:
                pl.when(outer)(lambda: far(2, k).wait_send())
                pl.when(inner)(lambda: passed(k).wait_send())
            else:
                far(b, k).wait_send()
        for a in range(1, n_seq):
            for b in range(n_voc):
                side(a, b, k).wait_send()
    for a in range(1, n_seq):
        pair_copy(a, my_s).wait_send()
    at = lax.broadcasted_iota(jnp.int32, (per, 2 * tokens), 1)
    at = jnp.where(at < tokens, at, at - tokens)
    index = place * per + lax.broadcasted_iota(jnp.int32, (per, 2 * tokens), 0)
    keep = at <= index
    counts = (index + 1).astype(F32)
    for n, (i, b) in enumerate(chips):
        stat_copy(n, logs[i] * n_voc + vocs[b]).wait_recv()

    lses, picks = merged(stat[...].reshape(n_log, n_voc, 2 * tokens), 1)
    signed = jnp.where(wide < tokens, -lses, picks)
    running = [jnp.sum(jnp.where(keep, signed[l], 0.0), axis=1, keepdims=True) / counts for l in range(n_log)]
    shifted = [prior[l] + running[l] for l in range(n_log)]
    highest = functools.reduce(jnp.maximum, shifted)
    mixture = highest + jnp.log(sum(jnp.exp(s - highest) for s in shifted))
    mine = running[0]
    for l in range(1, n_log):
        mine = jnp.where(my_l == l, running[l], mine)
    r8 = lax.broadcasted_iota(jnp.int32, (per, 2 * tokens), 0)
    c8 = lax.broadcasted_iota(jnp.int32, (per, 2 * tokens), 1)
    result = jnp.sum(jnp.where(r8 == c8, mine - mixture, 0.0), axis=0, keepdims=True)
    out_ref[...] = result[:, :per]

    for n in range(len(chips)):
        stat_copy(n, me).wait_send()


def fused(sizes, hidden, head_weight, logged_tokens, logger_share):
    n_log, n_seq, n_voc = sizes
    group = n_seq * n_voc
    per, depth = hidden.shape[1:]
    cols = head_weight.shape[2]
    tokens = logged_tokens.shape[0]
    vmem = pl.BlockSpec(memory_space=pltpu.VMEM)
    return pl.pallas_call(
        functools.partial(kernel, n_log, n_seq, n_voc),
        out_shape=pltpu.VMEM((1, per), F32),
        in_specs=[pl.BlockSpec(memory_space=pltpu.HBM)] * 4,
        out_specs=vmem,
        scratch_shapes=[
            pltpu.VMEM((group, per, depth), jnp.bfloat16),
            pltpu.VMEM((depth, cols), jnp.bfloat16),
            pltpu.VMEM((tokens, cols), F32),
            pltpu.VMEM((n_seq, 1, 2 * tokens), F32),
            pltpu.VMEM((n_log * n_voc, 1, 2 * tokens), F32),
            pltpu.VMEM((1, tokens), jnp.int32),
            pltpu.SMEM((n_log,), F32),
            pltpu.SemaphoreType.DMA((3,)),
            pltpu.SemaphoreType.DMA((CHUNKS,)),
            pltpu.SemaphoreType.DMA((group, CHUNKS)),
            pltpu.SemaphoreType.DMA((n_voc - 1, CHUNKS)),
            pltpu.SemaphoreType.DMA((n_seq - 1, n_voc, CHUNKS)),
            pltpu.SemaphoreType.DMA((n_seq,)),
            pltpu.SemaphoreType.DMA((n_seq,)),
            pltpu.SemaphoreType.DMA((n_log * n_voc,)),
            pltpu.SemaphoreType.DMA((n_log * n_voc,)),
        ],
        compiler_params=pltpu.CompilerParams(
            collective_id=0, has_side_effects=True, vmem_limit_bytes=63 * 2**20),
    )(logged_tokens.reshape(1, tokens), logger_share, hidden, head_weight)


def general(hidden, head_weight, logged_tokens, logger_share):
    axes = ("seq", "vocab")
    weight = head_weight[0]
    cols, per = weight.shape[1], hidden.shape[1]
    tokens = logged_tokens.shape[0]
    place = lax.axis_index(axes)
    logits = jnp.dot(lax.all_gather(hidden[0], axes, axis=0, tiled=True), weight, preferred_element_type=F32)
    top = jnp.max(logits, axis=1)
    total = jnp.sum(jnp.exp(logits - top[:, None]), axis=1)
    ids = place * cols + lax.broadcasted_iota(jnp.int32, (1, cols), 1)
    pick = jnp.sum(jnp.where(logged_tokens[:, None] == ids, logits, 0.0), axis=1)
    whole = lax.pmax(top, axes)
    total, pick = lax.psum((total * jnp.exp(top - whole), pick), axes)
    logp = pick - whole - jnp.log(total)
    mine = place * per + lax.broadcasted_iota(jnp.int32, (per, 1), 0)
    before = lax.broadcasted_iota(jnp.int32, (1, tokens), 1) <= mine
    running = jnp.sum(jnp.where(before, logp[None, :], 0.0), axis=1) / (mine[:, 0] + 1).astype(F32)
    every = lax.all_gather(running[None, :], "logger", axis=0, tiled=True)
    prior = jnp.log(logger_share) - jnp.log(jnp.sum(logger_share))
    shifted = prior[:, None] + every
    high = jnp.max(shifted, axis=0)
    mixture = high + jnp.log(jnp.sum(jnp.exp(shifted - high[None, :]), axis=0))
    return (running - mixture)[None, :]


def solution(mesh):
    sizes = tuple(mesh.shape[a] for a in ("logger", "seq", "vocab"))

    def on_device(hidden, head_weight, logged_tokens, logger_share):
        small = sizes[1:] == (2, 4) and 2 * logged_tokens.shape[0] == 128
        body = functools.partial(fused, sizes) if small else general
        return body(hidden, head_weight, logged_tokens, logger_share)

    return jax.shard_map(
        on_device,
        mesh=mesh,
        in_specs=(
            P("logger", ("seq", "vocab"), None),
            P("logger", None, ("seq", "vocab")),
            P(),
            P(),
        ),
        out_specs=P("logger", ("seq", "vocab")),
        check_vma=False,
    )
```
